32 devices in a mesh: age: 4 (over z), slab: 8 (over y, x, core).
Axes of the slice: x: 2, y: 2, z: 4, core: 2. Of those that a mesh axis runs over, the one named last changes fastest.
Arguments:
- velocity: float32 [3, 64, 128, 128], P(None, 'age', 'slab'), may hold values from -3 to 3
- mem_lm: float32 [64, 128, 128], P('age', 'slab'), may hold values from -0.5 to 1.5
- mem_mm: float32 [64, 128, 128], P('age', 'slab'), may hold values from 0.5 to 8
- send_ids: int32 [4, 8, 2, 64], P('age', 'slab'), may hold values from -1 to 255, as said below
- read_slot: int32 [4, 64, 128], P(None, 'age', 'slab'), may hold values from 0 to 383, as said below
- weights: float32 [8, 64, 128, 128], P(None, 'age', 'slab'), may hold values from 0 to 1, as said below
Outputs:
- new_lm: float32 [64, 128, 128], P('age', 'slab')
- new_mm: float32 [64, 128, 128], P('age', 'slab')
- viscosity: float32 [64, 128, 128], P('age', 'slab')
The draws below stay inside these ranges and needn't reach their ends.
Inputs may be any that keep to these rules, and one draw needn't show every extreme that they name: send_ids[g, s, 0] lists in ascending order, followed by -1, the distinct blocks of device (g, s) that the table of device (g, s+1) reads, all in its last 4 columns (j >= 12); send_ids[g, s, 1] likewise for device (g, s-1), all in its first 4 columns. The last device's direction 0 and the first device's direction 1 hold only -1. In every age group some list holds exactly 64 blocks. `read_slot`: A value r names a table line that holds a block: r < 256 an own block, otherwise a slot holding a block id in the list of the device below or above. The corner lines of a cell line are the blocks at rows max(i-1, 0) and max(i-1, 0) + 1 and at two neighbouring cells of the second dimension at most 4 cells away, inside the grid. The eight weights of a cell are the trilinear weights of three fractions, positive and summing to one.
All inputs are finite; a program needn't handle non-finite values.
Results may differ from the reference program's by a relative error of at most 0.0003.
Values sent between devices are 32-bit elements; how exact they have to be, the bound alone decides.
A program may use at most 64 MiB of HBM per device.

```python
import math
import jax
import jax.numpy as jnp
from jax import lax

CX = 16
CY = 16
NZ = 128
DMAX = 3
GROUPS = 4
PEERS = 8
NX = 64
NY = 128
CAP = 64


def departure_plan(key):
    key_up, key_amount, key_pick = jax.random.split(key, 3)
    device = jnp.arange(PEERS, dtype=jnp.int32)[None, :]
    chosen = jax.random.randint(key_pick, (GROUPS, 1), 0, PEERS)
    upward = jax.random.randint(key_up, (GROUPS, PEERS, CX), 0, 2)
    lifted = (device == PEERS - 1) | (device == chosen)
    full = lifted | (device == 0)
    upward = jnp.where(lifted[:, :, None], 1, upward)
    upward = jnp.where((device == 0)[:, :, None], 0, upward)
    amount = jax.random.randint(key_amount, (GROUPS, PEERS, CX, CY), 0, DMAX + 1)
    amount = jnp.where(full[:, :, None, None], DMAX, amount)
    row_index = jnp.arange(CX, dtype=jnp.int32)[:, None]
    column_index = jnp.arange(CY, dtype=jnp.int32)[None, :]
    low_row = jnp.maximum(row_index - 1, 0)
    first_y = jnp.where(upward[..., None] == 1, column_index - amount - 1, column_index + amount)
    sources = []
    blocks = []
    for across in range(2):
        for along in range(2):
            place = first_y + along
            source = jnp.where(place < 0, 1, jnp.where(place >= CY, 2, 0))
            column = place + CY * (place < 0).astype(jnp.int32) - CY * (place >= CY).astype(jnp.int32)
            block = (low_row + across) * CY + column
            sources.append(jnp.broadcast_to(source, (GROUPS, PEERS, CX, CY)))
            blocks.append(jnp.broadcast_to(block, (GROUPS, PEERS, CX, CY)))
    return (jnp.stack(sources, axis=2).astype(jnp.int32), jnp.stack(blocks, axis=2).astype(jnp.int32))


def needed(source, block, which):
    group_index = jnp.arange(GROUPS, dtype=jnp.int32)[:, None, None, None, None]
    peer_index = jnp.arange(PEERS, dtype=jnp.int32)[None, :, None, None, None]
    target = jnp.where(source == which, block, CX * CY)
    need = jnp.zeros((GROUPS, PEERS, CX * CY + 1), jnp.int32).at[group_index, peer_index, target].max(1)
    return need[..., :CX * CY]


def listing(need):
    ids = jnp.arange(CX * CY, dtype=jnp.int32)
    order = jnp.argsort(jnp.where(need == 1, ids, ids + CX * CY), axis=-1).astype(jnp.int32)[..., :CAP]
    count = jnp.sum(need, axis=-1, keepdims=True)
    return jnp.where(jnp.arange(CAP, dtype=jnp.int32) < count, order, -1).astype(jnp.int32)


def draw_send_ids(key, part):
    source, block = departure_plan(key)
    from_below = listing(needed(source, block, 1))
    from_above = listing(needed(source, block, 2))
    blank = jnp.full((GROUPS, 1, CAP), -1, jnp.int32)
    upward_list = jnp.concatenate([from_below[:, 1:], blank], axis=1)
    downward_list = jnp.concatenate([blank, from_above[:, :-1]], axis=1)
    return jnp.stack([upward_list, downward_list], axis=2).astype(jnp.int32)


def draw_read_slot(key, part):
    source, block = departure_plan(key)
    rank_below = jnp.cumsum(needed(source, block, 1), axis=-1) - 1
    rank_above = jnp.cumsum(needed(source, block, 2), axis=-1) - 1
    flat = block.reshape(GROUPS, PEERS, 4 * CX * CY)
    place_below = jnp.take_along_axis(rank_below, flat, axis=-1).reshape(source.shape)
    place_above = jnp.take_along_axis(rank_above, flat, axis=-1).reshape(source.shape)
    slot = jnp.where(source == 0, block, jnp.where(source == 1, CX * CY + place_below, CX * CY + CAP + place_above))
    return slot.transpose(2, 0, 3, 1, 4).reshape(4, NX, NY).astype(jnp.int32)


def draw_weights(key, part):
    key = jax.random.fold_in(key, 7)
    fraction = jax.random.uniform(key, (3, NX, NY, NZ), jnp.float32, 0.02, 0.98)
    corners = []
    for corner in range(8):
        value = jnp.ones((NX, NY, NZ), jnp.float32)
        for axis_number in range(3):
            upper = corner >> 2 - axis_number & 1
            factor = fraction[axis_number] if upper == 1 else 1.0 - fraction[axis_number]
            value = value * factor
        corners.append(value)
    return jnp.stack(corners).astype(jnp.float32)


def block_scale(rng, shape, cuts, low, largest):
    level, own = 1.0, jax.random.fold_in(rng, 6)
    for position, blocks in cuts:
        steps = jnp.exp(jax.random.uniform(jax.random.fold_in(own, position), (blocks,), jnp.float32, low / len(cuts), largest / len(cuts)))
        level = level * jnp.repeat(steps, shape[position] // blocks).reshape([-1 if axis == position else 1 for axis in range(len(shape))])
    return level


def scatter_about(key, dims, spread, bound, cuts=(), kind=jnp.bfloat16):
    entries = jax.random.normal(key, dims, jnp.float32) * spread
    if len(cuts) > 0:
        entries = block_scale(key, dims, cuts, -0.22, 0.18) * entries
    return jnp.clip(entries, min=-bound, max=bound).astype(kind)


def setup_inputs(seed: int = 0) -> dict:
    keys = jax.random.split(jax.random.key(seed), 7)
    velocity = scatter_about(keys[0], (3, NX, NY, NZ), 0.5, 3.0, ((1, 4), (2, 8)), jnp.float32)
    mem_lm = jnp.clip(-0.5 + 2.0 * jax.random.uniform(keys[1], (NX, NY, NZ), jnp.float32) ** block_scale(keys[1], (NX, NY, NZ), ((0, 4), (1, 8)), -0.2, 0.2), -0.5, 1.5)
    mem_mm = jnp.clip(jnp.exp(math.log(8.0) - 2.7725887 * jax.random.uniform(keys[2], (NX, NY, NZ), jnp.float32) ** block_scale(keys[2], (NX, NY, NZ), ((0, 4), (1, 8)), -0.2, 0.2)), 0.5, 8.0)
    send_ids = draw_send_ids(jax.random.fold_in(keys[6], 71), 0)
    read_slot = draw_read_slot(jax.random.fold_in(keys[6], 71), 0)
    weights = draw_weights(jax.random.fold_in(keys[6], 71), 0)
    return dict(velocity=velocity, mem_lm=mem_lm, mem_mm=mem_mm, send_ids=send_ids, read_slot=read_slot, weights=weights)


pair_list = ((0, 0), (1, 1), (2, 2), (0, 1), (0, 2), (1, 2))
time_step = 0.75
floor_value = 0.3

def smooth_valid(field):
    along_x = 0.25 * field[:-2] + 0.5 * field[1:-1] + 0.25 * field[2:]
    along_y = 0.25 * along_x[:, :-2] + 0.5 * along_x[:, 1:-1] + 0.25 * along_x[:, 2:]
    return 0.25 * jnp.roll(along_y, 1, axis=2) + 0.5 * along_y + 0.25 * jnp.roll(along_y, -1, axis=2)

def magnitude_of(parts):
    total = parts[0] * parts[0] + parts[1] * parts[1] + parts[2] * parts[2]
    total = total + 2.0 * (parts[3] * parts[3] + parts[4] * parts[4] + parts[5] * parts[5])
    return jnp.sqrt(2.0 * total + 1e-06)

def strain_parts(moved):
    along_x = 0.5 * (moved[:, 2:, 1:-1] - moved[:, :-2, 1:-1])
    along_y = 0.5 * (moved[:, 1:-1, 2:] - moved[:, 1:-1, :-2])
    middle = moved[:, 1:-1, 1:-1]
    along_z = 0.5 * (jnp.roll(middle, -1, axis=3) - jnp.roll(middle, 1, axis=3))
    slopes = (along_x, along_y, along_z)
    return [0.5 * (slopes[second][first] + slopes[first][second]) for first, second in pair_list]

def closure(moved, parts, magnitude):
    smooth_u = [smooth_valid(moved[comp]) for comp in range(3)]
    smooth_s = [smooth_valid(part) for part in parts]
    smooth_mag = magnitude_of(smooth_s)
    lm_total = jnp.zeros(smooth_mag.shape, jnp.float32)
    mm_total = jnp.zeros(smooth_mag.shape, jnp.float32)
    for place, (first, second) in enumerate(pair_list):
        factor = 1.0 if first == second else 2.0
        leonard = smooth_valid(moved[first] * moved[second]) - smooth_u[first] * smooth_u[second]
        model = 2.0 * (smooth_valid(magnitude * parts[place]) - 4.0 * smooth_mag * smooth_s[place])
        lm_total = lm_total + factor * leonard * model
        mm_total = mm_total + factor * model * model
    return (lm_total, mm_total)

def corner_sum(picked, corner_weights):
    total = jnp.zeros(corner_weights[..., 0, :, :].shape, jnp.float32)
    for corner in range(8):
        base = picked[..., corner >> 1, :, :]
        if corner & 1:
            base = jnp.roll(base, -1, axis=-1)
        total = total + corner_weights[..., corner, :, :] * base
    return total

def departed(mem_lm, mem_mm, send_ids, read_slot, weights):

    def to_rows(field):
        return field.reshape(GROUPS, CX, PEERS, CY, NZ).transpose(0, 2, 1, 3, 4).reshape(GROUPS, PEERS, CX * CY, NZ)
    lm_rows = to_rows(mem_lm)
    mm_rows = to_rows(mem_mm)
    slots = read_slot.reshape(4, GROUPS, CX, PEERS, CY).transpose(1, 3, 0, 2, 4).reshape(GROUPS, PEERS, 4, CX * CY)
    corner_weights = weights.reshape(8, GROUPS, CX, PEERS, CY, NZ).transpose(1, 3, 0, 2, 4, 5)
    corner_weights = corner_weights.reshape(GROUPS, PEERS, 8, CX * CY, NZ)

    def pick_rows(rows, index):
        return rows[index]

    def one_group(items):
        lm_group, mm_group, lists_group, slots_group, weight_group = items
        below_list = jnp.maximum(jnp.roll(lists_group[:, 0], 1, axis=0), 0).astype(jnp.int32)
        above_list = jnp.maximum(jnp.roll(lists_group[:, 1], -1, axis=0), 0).astype(jnp.int32)

        def table_of(rows):
            below = jax.vmap(pick_rows)(jnp.roll(rows, 1, axis=0), below_list)
            above = jax.vmap(pick_rows)(jnp.roll(rows, -1, axis=0), above_list)
            return jnp.concatenate([rows, below, above], axis=1)
        picked_lm = jax.vmap(pick_rows)(table_of(lm_group), slots_group)
        picked_mm = jax.vmap(pick_rows)(table_of(mm_group), slots_group)
        return (corner_sum(picked_lm, weight_group), corner_sum(picked_mm, weight_group))
    moved_lm, moved_mm = lax.map(one_group, (lm_rows, mm_rows, send_ids, slots, corner_weights))

    def to_grid(rows):
        return rows.reshape(GROUPS, PEERS, CX, CY, NZ).transpose(0, 2, 1, 3, 4).reshape(NX, NY, NZ)
    return (to_grid(moved_lm), to_grid(moved_mm))

def reference(velocity, mem_lm, mem_mm, send_ids, read_slot, weights):
    moved = jnp.pad(velocity, ((0, 0), (1, 1), (1, 1), (0, 0)))
    parts = strain_parts(moved)
    padded_parts = [jnp.pad(part, ((1, 1), (1, 1), (0, 0))) for part in parts]
    magnitude = magnitude_of(padded_parts)
    lm_local, mm_local = closure(moved, padded_parts, magnitude)
    own_magnitude = magnitude[1:-1, 1:-1]
    moved_lm, moved_mm = departed(mem_lm, mem_mm, send_ids, read_slot, weights)
    rate = time_step * jnp.maximum(jnp.maximum(moved_lm, 0.0) * moved_mm, floor_value) ** 0.125 / 1.5
    blend = rate / (1.0 + rate)
    new_lm = jnp.maximum(blend * lm_local + (1.0 - blend) * moved_lm, 0.0)
    new_mm = blend * mm_local + (1.0 - blend) * moved_mm
    viscosity = new_lm / new_mm * own_magnitude
    return (new_lm, new_mm, viscosity)
```

```python
import functools

import jax
import jax.numpy as jnp
from jax import lax
from jax.experimental import pallas as pl
from jax.experimental.pallas import tpu as pltpu
from jax.sharding import PartitionSpec as P

pair_list = ((0, 0), (1, 1), (2, 2), (0, 1), (0, 2), (1, 2))
time_step = 0.75
floor_value = 0.3
directions = tuple((dx, dy) for dx in (-1, 0, 1) for dy in (-1, 0, 1) if (dx, dy) != (0, 0))
reach = 4
pad_y = 8
MESH = pl.DeviceIdType.MESH


def halves(table):
    high = table.astype(jnp.bfloat16)
    low = (table - high.astype(jnp.float32)).astype(jnp.bfloat16)
    return jnp.concatenate([high, low], axis=0)


def root(value):
    return value * lax.rsqrt(value)


def kernel(
    vel, lm_in, mm_in, ids, slots_in, weights_in, out_lm, out_mm, out_visc,
    u, lm, mm, slots, w, raw, lists, picked, raws, mags, smooth,
    send_sems, recv_sems, local_sems,
):
    nx, ny, nz = lm.shape
    groups, peers = lax.axis_size("age"), lax.axis_size("slab")
    g, s = lax.axis_index("age"), lax.axis_index("slab")

    def has(dx, dy):
        ok = jnp.bool_(True)
        if dx < 0:
            ok = ok & (g > 0)
        if dx > 0:
            ok = ok & (g < groups - 1)
        if dy < 0:
            ok = ok & (s > 0)
        if dy > 0:
            ok = ok & (s < peers - 1)
        return ok

    own_vel = pltpu.make_async_copy(
        vel, u.at[:, pl.ds(2, nx), pl.ds(pad_y, ny), :], local_sems.at[0]
    )
    own_copies = [
        pltpu.make_async_copy(slots_in, slots, local_sems.at[1]),
        pltpu.make_async_copy(lm_in, lm, local_sems.at[2]),
        pltpu.make_async_copy(mm_in, mm, local_sems.at[3]),
    ]
    weight_copy = pltpu.make_async_copy(weights_in, w, local_sems.at[4])

    barrier = pltpu.get_barrier_semaphore()
    for dx, dy in directions:
        @pl.when(has(dx, dy))
        def _(dx=dx, dy=dy):
            pl.semaphore_signal(barrier, inc=1, device_id=(g + dx, s + dy), device_id_type=MESH)

    for copy in own_copies:
        copy.start()
    own_vel.start()
    weight_copy.start()

    zero = jnp.zeros((), jnp.float32)
    for dx, place in ((-1, 0), (1, nx + 2)):
        @pl.when(jnp.logical_not(has(dx, 0)))
        def _(place=place):
            u[:, place : place + 2, :, :] = jnp.zeros((3, 2) + u.shape[2:], jnp.float32)
    for dy, place in ((-1, pad_y - 2), (1, pad_y + ny)):
        @pl.when(jnp.logical_not(has(0, dy)))
        def _(dy=dy, place=place):
            u[:, :, place : place + 2, :] = jnp.zeros(u.shape[:2] + (2, nz), jnp.float32)
            side = 0 if dy < 0 else 1
            raw[:, :, side * reach : (side + 1) * reach, :] = jnp.zeros((2, nx, reach, nz), jnp.float32)
            lists[side] = jnp.full(lists.shape[1:], -1, jnp.int32)

    def span(step, cells, begin):
        if step == 0:
            return pl.ds(0, cells), pl.ds(begin, cells)
        if step > 0:
            return pl.ds(cells - 2, 2), pl.ds(begin - 2, 2)
        return pl.ds(0, 2), pl.ds(begin + cells, 2)

    def remote(source, target, place, dx, dy):
        return pltpu.make_async_remote_copy(
            src_ref=source, dst_ref=target, send_sem=send_sems.at[place],
            recv_sem=recv_sems.at[place], device_id=(g + dx, s + dy), device_id_type=MESH,
        )

    halo = []
    for place, (dx, dy) in enumerate(directions):
        from_x, to_x = span(dx, nx, 2)
        from_y, to_y = span(dy, ny, pad_y)
        halo.append((
            dx, dy,
            remote(vel.at[:, from_x, from_y, :], u.at[:, to_x, to_y, :], place, dx, dy),
        ))
    memory = []
    place = len(directions)
    for dy in (1, -1):
        side = 0 if dy > 0 else 1
        columns = pl.ds(ny - reach, reach) if dy > 0 else pl.ds(0, reach)
        for number, field in enumerate((lm_in, mm_in)):
            memory.append((0, dy, remote(
                field.at[:, columns, :], raw.at[number, :, pl.ds(side * reach, reach), :], place, 0, dy
            )))
            place += 1
        memory.append((0, dy, remote(ids.at[0, 0], lists.at[side], place, 0, dy)))
        place += 1

    incoming = (
        ((g > 0).astype(jnp.int32) + (g < groups - 1).astype(jnp.int32) + 1)
        * ((s > 0).astype(jnp.int32) + (s < peers - 1).astype(jnp.int32) + 1)
        - 1
    )
    pl.semaphore_wait(barrier, incoming)
    for dx, dy, copy in halo + memory:
        @pl.when(has(dx, dy))
        def _(copy=copy):
            copy.start()

    for copy in own_copies:
        copy.wait()
    lines = 4 * nx
    blocks = nx * ny
    eye = lax.broadcasted_iota(jnp.int32, (1, ny, ny), 1) == lax.broadcasted_iota(jnp.int32, (1, ny, ny), 2)
    slot_rows = slots[...].astype(jnp.float32).reshape(lines, 1, ny)
    slot_column = jnp.sum(jnp.where(eye, slot_rows, 0.0), axis=2, keepdims=True)

    def one_hot(begin, count):
        ids_of = (lax.broadcasted_iota(jnp.int32, (1, 1, count), 2) + begin).astype(jnp.float32)
        hot = jnp.where(slot_column == ids_of, 1.0, 0.0)
        hot = hot.reshape(lines * ny, count).astype(jnp.bfloat16)
        return jnp.concatenate([hot, hot], axis=1)

    own_table = jnp.concatenate([lm[...].reshape(blocks, nz), mm[...].reshape(blocks, nz)], axis=1)
    picked[...] = jnp.dot(one_hot(0, blocks), halves(own_table), preferred_element_type=jnp.float32)

    own_vel.wait()
    for dx, dy, copy in halo:
        @pl.when(has(-dx, -dy))
        def _(copy=copy):
            copy.wait_recv()

    rows = raws.shape[1]
    row = lax.broadcasted_iota(jnp.int32, (rows, nz), 0)
    inside_low = jnp.where((row > 0) | (s > 0), 1.0, 0.0)
    inside = jnp.where((row < ny + 1) | (s < peers - 1), inside_low, 0.0)

    def strain_step(e, carry):
        shift = e // 1024
        def get(comp, along_x, along_y, count=rows):
            return u[comp, e + 1 + along_x, pl.ds(pad_y - 1 + along_y + shift, count), :]
        center = [get(comp, 0, 0) for comp in range(3)]
        slopes = [
            [get(comp, 1, 0) - get(comp, -1, 0) for comp in range(3)],
            [get(comp, 0, 1) - get(comp, 0, -1) for comp in range(3)],
            [pltpu.roll(center[comp], nz - 1, 1) - pltpu.roll(center[comp], 1, 1) for comp in range(3)],
        ]
        within = jnp.where(((e > 0) | (g > 0)) & ((e < nx + 1) | (g < groups - 1)), 1.0, 0.0)
        mask = inside * within
        parts = [(slopes[b][a] + slopes[a][b]) * mask for a, b in pair_list]
        total = parts[0] * parts[0] + parts[1] * parts[1] + parts[2] * parts[2]
        total = total + 2.0 * (parts[3] * parts[3] + parts[4] * parts[4] + parts[5] * parts[5])
        mag = root(total * 0.125 + 1e-06)
        mags[e] = mag
        for place in range(6):
            a, b = pair_list[place]
            raws[place] = parts[place]
            raws[6 + place] = mag * parts[place]
            raws[12 + place] = center[a] * center[b]
        for place in range(18):
            below = raws[place, pl.ds(shift, ny), :]
            middle = raws[place, pl.ds(shift + 1, ny), :]
            above = raws[place, pl.ds(shift + 2, ny), :]
            smooth[place, e] = (below + above) + (middle + middle)
        for comp in range(3):
            middle = get(comp, 0, 1, ny)
            smooth[18 + comp, e] = (get(comp, 0, 0, ny) + get(comp, 0, 2, ny)) + (middle + middle)
        return carry

    lax.fori_loop(0, nx + 2, strain_step, 0)

    for dx, dy, copy in memory:
        @pl.when(has(-dx, -dy))
        def _(copy=copy):
            copy.wait_recv()
    strip = nx * 2 * reach
    near = jnp.concatenate([raw[0].reshape(strip, nz), raw[1].reshape(strip, nz)], axis=1)
    near = halves(near)
    capacity = lists.shape[2]
    line = lax.broadcasted_iota(jnp.int32, (strip, capacity), 0)
    column = line % (2 * reach)
    line_row = line // (2 * reach)
    below_id = jnp.where(column < reach, line_row * ny + (ny - reach) + column, -5)
    above_id = jnp.where(column >= reach, line_row * ny + column - reach, -5)
    listed = []
    for side, block_id in ((0, below_id), (1, above_id)):
        hot = jnp.where(block_id == lists[side, side : side + 1, :], 1.0, 0.0).astype(jnp.bfloat16)
        hot = jnp.concatenate([hot, hot], axis=0)
        listed.append(lax.dot_general(hot, near, (((0,), (0,)), ((), ())), preferred_element_type=jnp.float32))
    far_table = halves(jnp.concatenate(listed, axis=0))
    picked[...] += jnp.dot(one_hot(blocks, 2 * capacity), far_table, preferred_element_type=jnp.float32)
    weight_copy.wait()

    def final_step(x, carry):
        shift = x // 1024
        def filtered(place):
            f = (smooth[place, x] + smooth[place, x + 2]) + 2.0 * smooth[place, x + 1]
            f = f + pltpu.roll(f, 1, 1)
            return f + pltpu.roll(f, nz - 1, 1)
        flow = [0.125 * filtered(18 + comp) for comp in range(3)]
        parts = [filtered(place) for place in range(6)]
        total = parts[0] * parts[0] + parts[1] * parts[1] + parts[2] * parts[2]
        total = total + 2.0 * (parts[3] * parts[3] + parts[4] * parts[4] + parts[5] * parts[5])
        mag4 = 4.0 * root(total * (2.0 / 65536.0) + 1e-06)
        lm_sum, mm_sum = [], []
        for half in (range(3), range(3, 6)):
            lm_part = mm_part = None
            for place in half:
                a, b = pair_list[place]
                leonard = filtered(12 + place) - flow[a] * flow[b]
                model = filtered(6 + place) - mag4 * parts[place]
                lm_part = leonard * model if lm_part is None else lm_part + leonard * model
                mm_part = model * model if mm_part is None else mm_part + model * model
            lm_sum.append(lm_part)
            mm_sum.append(mm_part)
        lm_local = (lm_sum[0] + 2.0 * lm_sum[1]) * (1.0 / 8192.0)
        mm_local = (mm_sum[0] + 2.0 * mm_sum[1]) * (1.0 / 16384.0)
        moved = [None, None]
        for corner in range(4):
            low, high = w[2 * corner, x], w[2 * corner + 1, x]
            start = pl.multiple_of((corner * nx + x) * ny, ny)
            for field in range(2):
                base = picked[pl.ds(start, ny), field * nz : (field + 1) * nz]
                term = low * base + high * pltpu.roll(base, nz - 1, 1)
                moved[field] = term if moved[field] is None else moved[field] + term
        moved_lm, moved_mm = moved
        power = root(root(root(jnp.maximum(jnp.maximum(moved_lm, 0.0) * moved_mm, floor_value))))
        rate = (time_step / 1.5) * power
        blend = rate / (1.0 + rate)
        new_lm = jnp.maximum(moved_lm + blend * (lm_local - moved_lm), 0.0)
        new_mm = moved_mm + blend * (mm_local - moved_mm)
        out_lm[x] = new_lm
        out_mm[x] = new_mm
        out_visc[x] = new_lm / new_mm * mags[x + 1, pl.ds(1 + shift, ny), :]
        return carry

    lax.fori_loop(0, nx, final_step, 0)

    for dx, dy, copy in halo + memory:
        @pl.when(has(dx, dy))
        def _(copy=copy):
            copy.wait_send()


def on_device(velocity, mem_lm, mem_mm, send_ids, read_slot, weights):
    nx, ny, nz = mem_lm.shape
    capacity = send_ids.shape[3]
    f32 = jnp.float32
    rows = ny + 8
    out = jax.ShapeDtypeStruct(mem_lm.shape, f32)
    copies = len(directions) + 6
    return pl.pallas_call(
        kernel,
        out_shape=(out, out, out),
        in_specs=[pl.BlockSpec(memory_space=pl.ANY)] * 6,
        out_specs=[pl.BlockSpec(memory_space=pltpu.VMEM)] * 3,
        scratch_shapes=[
            pltpu.VMEM((3, nx + 4, ny + 2 * pad_y, nz), f32),
            pltpu.VMEM(mem_lm.shape, f32),
            pltpu.VMEM(mem_lm.shape, f32),
            pltpu.VMEM(read_slot.shape, jnp.int32),
            pltpu.VMEM(weights.shape, f32),
            pltpu.VMEM((2, nx, 2 * reach, nz), f32),
            pltpu.VMEM((2, 2, capacity), jnp.int32),
            pltpu.VMEM((4 * nx * ny, 2 * nz), f32),
            pltpu.VMEM((18, rows, nz), f32),
            pltpu.VMEM((nx + 2, rows, nz), f32),
            pltpu.VMEM((21, nx + 2, ny, nz), f32),
            pltpu.SemaphoreType.DMA((copies,)),
            pltpu.SemaphoreType.DMA((copies,)),
            pltpu.SemaphoreType.DMA((5,)),
        ],
        compiler_params=pltpu.CompilerParams(
            collective_id=0, has_side_effects=True, vmem_limit_bytes=48 << 20
        ),
    )(velocity, mem_lm, mem_mm, send_ids, read_slot, weights)


def solution(mesh):
    return jax.shard_map(
        on_device,
        mesh=mesh,
        in_specs=(
            P(None, "age", "slab", None),
            P("age", "slab", None),
            P("age", "slab", None),
            P("age", "slab", None, None),
            P(None, "age", "slab"),
            P(None, "age", "slab", None),
        ),
        out_specs=(P("age", "slab", None), P("age", "slab", None), P("age", "slab", None)),
        check_vma=False,
    )
```

```python
import jax
import jax.numpy as jnp
from jax import lax
from jax.experimental import pallas as pl
from jax.experimental.pallas import tpu as pltpu
from jax.sharding import PartitionSpec as P

pair_list = ((0, 0), (1, 1), (2, 2), (0, 1), (0, 2), (1, 2))
time_step = 0.75
floor_value = 0.3
directions = tuple((dx, dy) for dx in (-1, 0, 1) for dy in (-1, 0, 1) if (dx, dy) != (0, 0))
reach = 4
pad_y = 8
MESH = pl.DeviceIdType.MESH


def halves(table):
    high = table.astype(jnp.bfloat16)
    low = (table - high.astype(jnp.float32)).astype(jnp.bfloat16)
    return jnp.concatenate([high, low], axis=0)


def root(value):
    return value * lax.rsqrt(value)


def kernel(
    vel, lm_in, mm_in, ids, slots_in, weights_in, new_lm_out, new_mm_out, visc_out,
    u, lm, mm, slots, w, raw, lists, picked, far_picked, own_moved, raws, mags, smooth, outs,
    send_sems, recv_sems, local_sems, out_sems,
):
    nx, ny, nz = lm.shape
    groups, peers = lax.axis_size("age"), lax.axis_size("slab")
    g, s = lax.axis_index("age"), lax.axis_index("slab")

    def has(dx, dy):
        ok = jnp.bool_(True)
        if dx < 0:
            ok = ok & (g > 0)
        if dx > 0:
            ok = ok & (g < groups - 1)
        if dy < 0:
            ok = ok & (s > 0)
        if dy > 0:
            ok = ok & (s < peers - 1)
        return ok

    own_vel = pltpu.make_async_copy(
        vel, u.at[:, pl.ds(2, nx), pl.ds(pad_y, ny), :], local_sems.at[0]
    )
    own_copies = [
        pltpu.make_async_copy(slots_in, slots, local_sems.at[1]),
        pltpu.make_async_copy(lm_in, lm, local_sems.at[2]),
        pltpu.make_async_copy(mm_in, mm, local_sems.at[3]),
    ]
    weight_copy = pltpu.make_async_copy(weights_in, w, local_sems.at[4])

    barrier = pltpu.get_barrier_semaphore()
    for dx, dy in directions:
        @pl.when(has(dx, dy))
        def _(dx=dx, dy=dy):
            pl.semaphore_signal(barrier, inc=1, device_id=(g + dx, s + dy), device_id_type=MESH)

    for copy in own_copies:
        copy.start()
    own_vel.start()
    weight_copy.start()

    zero = jnp.zeros((), jnp.float32)
    for dx, place in ((-1, 0), (1, nx + 2)):
        @pl.when(jnp.logical_not(has(dx, 0)))
        def _(place=place):
            u[:, place : place + 2, :, :] = jnp.zeros((3, 2) + u.shape[2:], jnp.float32)
    for dy, place in ((-1, pad_y - 2), (1, pad_y + ny)):
        @pl.when(jnp.logical_not(has(0, dy)))
        def _(dy=dy, place=place):
            u[:, :, place : place + 2, :] = jnp.zeros(u.shape[:2] + (2, nz), jnp.float32)
            side = 0 if dy < 0 else 1
            raw[:, :, side * reach : (side + 1) * reach, :] = jnp.zeros((2, nx, reach, nz), jnp.float32)
            lists[side] = jnp.full(lists.shape[1:], -1, jnp.int32)

    def span(step, cells, begin):
        if step == 0:
            return pl.ds(0, cells), pl.ds(begin, cells)
        if step > 0:
            return pl.ds(cells - 2, 2), pl.ds(begin - 2, 2)
        return pl.ds(0, 2), pl.ds(begin + cells, 2)

    def remote(source, target, place, dx, dy):
        return pltpu.make_async_remote_copy(
            src_ref=source, dst_ref=target, send_sem=send_sems.at[place],
            recv_sem=recv_sems.at[place], device_id=(g + dx, s + dy), device_id_type=MESH,
        )

    halo = []
    for place, (dx, dy) in enumerate(directions):
        from_x, to_x = span(dx, nx, 2)
        from_y, to_y = span(dy, ny, pad_y)
        halo.append((
            dx, dy,
            remote(vel.at[:, from_x, from_y, :], u.at[:, to_x, to_y, :], place, dx, dy),
        ))
    memory = []
    place = len(directions)
    for dy in (1, -1):
        side = 0 if dy > 0 else 1
        columns = pl.ds(ny - reach, reach) if dy > 0 else pl.ds(0, reach)
        for number, field in enumerate((lm_in, mm_in)):
            memory.append((0, dy, remote(
                field.at[:, columns, :], raw.at[number, :, pl.ds(side * reach, reach), :], place, 0, dy
            )))
            place += 1
        memory.append((0, dy, remote(ids.at[0, 0], lists.at[side], place, 0, dy)))
        place += 1

    incoming = (
        ((g > 0).astype(jnp.int32) + (g < groups - 1).astype(jnp.int32) + 1)
        * ((s > 0).astype(jnp.int32) + (s < peers - 1).astype(jnp.int32) + 1)
        - 1
    )
    pl.semaphore_wait(barrier, incoming)
    for dx, dy, copy in halo + memory:
        @pl.when(has(dx, dy))
        def _(copy=copy):
            copy.start()

    for copy in own_copies:
        copy.wait()
    lines = 4 * nx
    blocks = nx * ny
    slot_rows = slots[...].astype(jnp.float32).reshape(lines, 1, ny)
    lane = lax.broadcasted_iota(jnp.int32, (1, ny, ny), 2)
    edge_row = lax.broadcasted_iota(jnp.int32, (1, 2 * reach, ny), 1)
    edge_row = jnp.where(edge_row < reach, edge_row, edge_row + ny - 2 * reach)

    def slot_column(wanted):
        picks = jnp.where(lane[:, : wanted.shape[1]] == wanted, slot_rows, 0.0)
        return jnp.sum(picks, axis=2, keepdims=True)

    def one_hot(column, begin, count):
        ids_of = (lax.broadcasted_iota(jnp.int32, (1, 1, count), 2) + begin).astype(jnp.float32)
        hot = jnp.where(column == ids_of, 1.0, 0.0)
        hot = hot.reshape(lines * column.shape[1], count).astype(jnp.bfloat16)
        return jnp.concatenate([hot, hot], axis=1)

    own_table = jnp.concatenate([lm[...].reshape(blocks, nz), mm[...].reshape(blocks, nz)], axis=1)
    own_hot = one_hot(slot_column(lax.broadcasted_iota(jnp.int32, (1, ny, ny), 1)), 0, blocks)
    picked[...] = jnp.dot(own_hot, halves(own_table), preferred_element_type=jnp.float32)
    capacity = lists.shape[2]
    far_hot = one_hot(slot_column(edge_row), blocks, 2 * capacity)
    weight_copy.wait()

    def own_step(x, carry):
        for half in range(ny // 8):
            moved = [None, None]
            for corner in range(4):
                low = w[2 * corner, x, half * 8 : half * 8 + 8, :]
                high = w[2 * corner + 1, x, half * 8 : half * 8 + 8, :]
                start = pl.multiple_of((corner * nx + x) * ny, ny) + half * 8
                for field in range(2):
                    base = picked[pl.ds(pl.multiple_of(start, 8), 8), field * nz : (field + 1) * nz]
                    term = low * base + high * pltpu.roll(base, nz - 1, 1)
                    moved[field] = term if moved[field] is None else moved[field] + term
            for field in range(2):
                own_moved[field, x, half * 8 : half * 8 + 8, :] = moved[field]
        return carry

    lax.fori_loop(0, nx, own_step, 0)

    own_vel.wait()
    for dx, dy, copy in halo:
        @pl.when(has(-dx, -dy))
        def _(copy=copy):
            copy.wait_recv()

    row = lax.broadcasted_iota(jnp.int32, (8, nz), 0)
    chunks = raws.shape[2] // 8
    insides = []
    for chunk in range(chunks):
        low = jnp.where((row + 8 * chunk > 0) | (s > 0), 1.0, 0.0)
        insides.append(jnp.where((row + 8 * chunk < ny + 1) | (s < peers - 1), low, 0.0))

    def strain_at(e, slot):
        shift = e // 1024
        within = jnp.where(((e > 0) | (g > 0)) & ((e < nx + 1) | (g < groups - 1)), 1.0, 0.0)
        def get(comp, along_x, along_y, count):
            return u[comp, e + 1 + along_x, pl.ds(pad_y - 1 + along_y + shift, count), :]
        for chunk in range(chunks):
            k = 8 * chunk
            center = [get(comp, 0, k, 8) for comp in range(3)]
            slopes = [
                [get(comp, 1, k, 8) - get(comp, -1, k, 8) for comp in range(3)],
                [get(comp, 0, k + 1, 8) - get(comp, 0, k - 1, 8) for comp in range(3)],
                [pltpu.roll(center[comp], nz - 1, 1) - pltpu.roll(center[comp], 1, 1) for comp in range(3)],
            ]
            mask = insides[chunk] * within
            parts = [(slopes[b][a] + slopes[a][b]) * mask for a, b in pair_list]
            total = parts[0] * parts[0] + parts[1] * parts[1] + parts[2] * parts[2]
            total = total + 2.0 * (parts[3] * parts[3] + parts[4] * parts[4] + parts[5] * parts[5])
            mag = root(total * 0.125 + 1e-06)
            mags[e, k : k + 8, :] = mag
            for place in range(6):
                a, b = pair_list[place]
                raws[slot, place, k : k + 8, :] = parts[place]
                raws[slot, 6 + place, k : k + 8, :] = mag * parts[place]
                raws[slot, 12 + place, k : k + 8, :] = center[a] * center[b]
        for place in range(18):
            below = raws[slot, place, pl.ds(shift, ny), :]
            middle = raws[slot, place, pl.ds(shift + 1, ny), :]
            above = raws[slot, place, pl.ds(shift + 2, ny), :]
            smooth[place, e] = (below + above) + (middle + middle)
        for comp in range(3):
            middle = get(comp, 0, 1, ny)
            smooth[18 + comp, e] = (get(comp, 0, 0, ny) + get(comp, 0, 2, ny)) + (middle + middle)

    def strain_step(i, carry):
        for slot in range(raws.shape[0]):
            strain_at(i * raws.shape[0] + slot, slot)
        return carry

    lax.fori_loop(0, (nx + 2) // raws.shape[0], strain_step, 0)

    for dx, dy, copy in memory:
        @pl.when(has(-dx, -dy))
        def _(copy=copy):
            copy.wait_recv()
    strip = nx * 2 * reach
    near = jnp.concatenate([raw[0].reshape(strip, nz), raw[1].reshape(strip, nz)], axis=1)
    near = halves(near)
    line = lax.broadcasted_iota(jnp.int32, (strip, capacity), 0)
    column = line % (2 * reach)
    line_row = line // (2 * reach)
    below_id = jnp.where(column < reach, line_row * ny + (ny - reach) + column, -5)
    above_id = jnp.where(column >= reach, line_row * ny + column - reach, -5)
    listed = []
    for side, block_id in ((0, below_id), (1, above_id)):
        hot = jnp.where(block_id == lists[side, side : side + 1, :], 1.0, 0.0).astype(jnp.bfloat16)
        hot = jnp.concatenate([hot, hot], axis=0)
        listed.append(lax.dot_general(hot, near, (((0,), (0,)), ((), ())), preferred_element_type=jnp.float32))
    far_table = halves(jnp.concatenate(listed, axis=0))
    far_picked[...] = jnp.dot(far_hot, far_table, preferred_element_type=jnp.float32)
    edge_low = lax.broadcasted_iota(jnp.int32, (8, nz), 0) < reach

    def final_step(x, carry):
        shift = x // 1024
        def filtered(half, place):
            ys = slice(half * 8, half * 8 + 8)
            f = (smooth[place, x, ys] + smooth[place, x + 2, ys]) + 2.0 * smooth[place, x + 1, ys]
            return (pltpu.roll(f, 1, 1) + pltpu.roll(f, nz - 1, 1)) + (f + f)
        far = [None, None]
        for corner in range(4):
            low = jnp.where(edge_low, w[2 * corner, x, 0:8, :], w[2 * corner, x, ny - 8 : ny, :])
            high = jnp.where(edge_low, w[2 * corner + 1, x, 0:8, :], w[2 * corner + 1, x, ny - 8 : ny, :])
            start = pl.multiple_of((corner * nx + x) * 8, 8)
            for field in range(2):
                base = far_picked[pl.ds(start, 8), field * nz : (field + 1) * nz]
                term = low * base + high * pltpu.roll(base, nz - 1, 1)
                far[field] = term if far[field] is None else far[field] + term
        for half in range(ny // 8):
            ys = slice(half * 8, half * 8 + 8)
            def keep(value):
                return jnp.where(edge_low, value, 0.0) if half == 0 else jnp.where(edge_low, 0.0, value)
            flow = [0.125 * filtered(half, 18 + comp) for comp in range(3)]
            parts = [filtered(half, place) for place in range(6)]
            total = parts[0] * parts[0] + parts[1] * parts[1] + parts[2] * parts[2]
            total = total + 2.0 * (parts[3] * parts[3] + parts[4] * parts[4] + parts[5] * parts[5])
            mag4 = 4.0 * root(total * (2.0 / 65536.0) + 1e-06)
            lm_sum, mm_sum = [], []
            for group in (range(3), range(3, 6)):
                lm_part = mm_part = None
                for place in group:
                    a, b = pair_list[place]
                    leonard = filtered(half, 12 + place) - flow[a] * flow[b]
                    model = filtered(half, 6 + place) - mag4 * parts[place]
                    lm_part = leonard * model if lm_part is None else lm_part + leonard * model
                    mm_part = model * model if mm_part is None else mm_part + model * model
                lm_sum.append(lm_part)
                mm_sum.append(mm_part)
            lm_local = (lm_sum[0] + 2.0 * lm_sum[1]) * (1.0 / 8192.0)
            mm_local = (mm_sum[0] + 2.0 * mm_sum[1]) * (1.0 / 16384.0)
            moved_lm = own_moved[0, x, ys, :] + keep(far[0])
            moved_mm = own_moved[1, x, ys, :] + keep(far[1])
            power = root(root(root(jnp.maximum(jnp.maximum(moved_lm, 0.0) * moved_mm, floor_value))))
            rate = (time_step / 1.5) * power
            blend = rate / (1.0 + rate)
            new_lm = jnp.maximum(moved_lm + blend * (lm_local - moved_lm), 0.0)
            new_mm = moved_mm + blend * (mm_local - moved_mm)
            outs[0, x, ys, :] = new_lm
            outs[1, x, ys, :] = new_mm
            outs[2, x, ys, :] = new_lm / new_mm * mags[x + 1, pl.ds(half * 8 + 1 + shift, 8), :]
        return carry

    sent = []
    unroll = nx // 2
    for part in range(2):
        strip_x = pl.ds(part * (nx // 2), nx // 2)
        lax.fori_loop(part * (nx // 2), (part + 1) * (nx // 2), final_step, 0, unroll=unroll)
        for place, target in enumerate((new_lm_out, new_mm_out, visc_out)):
            copy = pltpu.make_async_copy(outs.at[place, strip_x], target.at[strip_x], out_sems.at[part, place])
            copy.start()
            sent.append(copy)

    for dx, dy, copy in halo + memory:
        @pl.when(has(dx, dy))
        def _(copy=copy):
            copy.wait_send()
    for copy in sent:
        copy.wait()


def hand_over(a_in, b_in, c_in, a_out, b_out, c_out):
    a_out[...] = a_in[...]
    b_out[...] = b_in[...]
    c_out[...] = c_in[...]


def on_device(velocity, mem_lm, mem_mm, send_ids, read_slot, weights):
    nx, ny, nz = mem_lm.shape
    capacity = send_ids.shape[3]
    f32 = jnp.float32
    rows = ny + 8
    out = jax.ShapeDtypeStruct(mem_lm.shape, f32)
    copies = len(directions) + 6
    fields = pl.pallas_call(
        kernel,
        out_shape=(out, out, out),
        in_specs=[pl.BlockSpec(memory_space=pltpu.HBM)] * 6,
        out_specs=[pl.BlockSpec(memory_space=pltpu.HBM)] * 3,
        scratch_shapes=[
            pltpu.VMEM((3, nx + 4, ny + 2 * pad_y, nz), f32),
            pltpu.VMEM(mem_lm.shape, f32),
            pltpu.VMEM(mem_lm.shape, f32),
            pltpu.VMEM(read_slot.shape, jnp.int32),
            pltpu.VMEM(weights.shape, f32),
            pltpu.VMEM((2, nx, 2 * reach, nz), f32),
            pltpu.VMEM((2, 2, capacity), jnp.int32),
            pltpu.VMEM((4 * nx * ny, 2 * nz), f32),
            pltpu.VMEM((4 * nx * 2 * reach, 2 * nz), f32),
            pltpu.VMEM((2,) + mem_lm.shape, f32),
            pltpu.VMEM((3, 18, rows, nz), f32),
            pltpu.VMEM((nx + 2, rows, nz), f32),
            pltpu.VMEM((21, nx + 2, ny, nz), f32),
            pltpu.VMEM((3,) + mem_lm.shape, f32),
            pltpu.SemaphoreType.DMA((copies,)),
            pltpu.SemaphoreType.DMA((copies,)),
            pltpu.SemaphoreType.DMA((5,)),
            pltpu.SemaphoreType.DMA((2, 3)),
        ],
        compiler_params=pltpu.CompilerParams(
            collective_id=0, has_side_effects=True, vmem_limit_bytes=60 << 20
        ),
    )(velocity, mem_lm, mem_mm, send_ids, read_slot, weights)
    return pl.pallas_call(
        hand_over,
        out_shape=(out, out, out),
        in_specs=[pl.BlockSpec(memory_space=pltpu.VMEM)] * 3,
        out_specs=[pl.BlockSpec(memory_space=pltpu.VMEM)] * 3,
        compiler_params=pltpu.CompilerParams(vmem_limit_bytes=60 << 20),
    )(*fields)


def solution(mesh):
    return jax.shard_map(
        on_device,
        mesh=mesh,
        in_specs=(
            P(None, "age", "slab", None),
            P("age", "slab", None),
            P("age", "slab", None),
            P("age", "slab", None, None),
            P(None, "age", "slab"),
            P(None, "age", "slab", None),
        ),
        out_specs=(P("age", "slab", None), P("age", "slab", None), P("age", "slab", None)),
        check_vma=False,
    )
```

```python
import jax
import jax.numpy as jnp
from jax import lax
from jax.experimental import pallas as pl
from jax.experimental.pallas import tpu as pltpu
from jax.sharding import PartitionSpec as P

pair_list = ((0, 0), (1, 1), (2, 2), (0, 1), (0, 2), (1, 2))
time_step = 0.75
floor_value = 0.3
directions = tuple((dx, dy) for dx in (-1, 0, 1) for dy in (-1, 0, 1) if (dx, dy) != (0, 0))
reach = 4
pad_y = 8
MESH = pl.DeviceIdType.MESH


def halves(table):
    high = table.astype(jnp.bfloat16)
    low = (table - high.astype(jnp.float32)).astype(jnp.bfloat16)
    return jnp.concatenate([high, low], axis=0)


def root(value):
    return value * lax.rsqrt(value)


def kernel(
    vel, lm_in, mm_in, ids, slots_in, weights_in, new_lm_out, new_mm_out, visc_out,
    u, lm, mm, slots, w, raw, lists, picked, far_picked, own_moved, raws, mags, smooth, outs,
    send_sems, recv_sems, local_sems, out_sems,
):
    nx, ny, nz = lm.shape
    groups, peers = lax.axis_size("age"), lax.axis_size("slab")
    g, s = lax.axis_index("age"), lax.axis_index("slab")

    def has(dx, dy):
        ok = jnp.bool_(True)
        if dx < 0:
            ok = ok & (g > 0)
        if dx > 0:
            ok = ok & (g < groups - 1)
        if dy < 0:
            ok = ok & (s > 0)
        if dy > 0:
            ok = ok & (s < peers - 1)
        return ok

    own_vel = pltpu.make_async_copy(
        vel, u.at[:, pl.ds(2, nx), pl.ds(pad_y, ny), :], local_sems.at[0]
    )
    own_copies = [
        pltpu.make_async_copy(slots_in, slots, local_sems.at[1]),
        pltpu.make_async_copy(lm_in, lm, local_sems.at[2]),
        pltpu.make_async_copy(mm_in, mm, local_sems.at[3]),
    ]
    weight_copy = pltpu.make_async_copy(weights_in, w, local_sems.at[4])

    barrier = pltpu.get_barrier_semaphore()
    for dx, dy in directions:
        @pl.when(has(dx, dy))
        def _(dx=dx, dy=dy):
            pl.semaphore_signal(barrier, inc=1, device_id=(g + dx, s + dy), device_id_type=MESH)

    for copy in own_copies:
        copy.start()
    own_vel.start()
    weight_copy.start()

    zero = jnp.zeros((), jnp.float32)
    for dx, place in ((-1, 0), (1, nx + 2)):
        @pl.when(jnp.logical_not(has(dx, 0)))
        def _(place=place):
            u[:, place : place + 2, :, :] = jnp.zeros((3, 2) + u.shape[2:], jnp.float32)
    for dy, place in ((-1, pad_y - 2), (1, pad_y + ny)):
        @pl.when(jnp.logical_not(has(0, dy)))
        def _(dy=dy, place=place):
            u[:, :, place : place + 2, :] = jnp.zeros(u.shape[:2] + (2, nz), jnp.float32)
            side = 0 if dy < 0 else 1
            raw[:, :, side * reach : (side + 1) * reach, :] = jnp.zeros((2, nx, reach, nz), jnp.float32)
            lists[side] = jnp.full(lists.shape[1:], -1, jnp.int32)

    def span(step, cells, begin):
        if step == 0:
            return pl.ds(0, cells), pl.ds(begin, cells)
        if step > 0:
            return pl.ds(cells - 2, 2), pl.ds(begin - 2, 2)
        return pl.ds(0, 2), pl.ds(begin + cells, 2)

    def remote(source, target, place, dx, dy):
        return pltpu.make_async_remote_copy(
            src_ref=source, dst_ref=target, send_sem=send_sems.at[place],
            recv_sem=recv_sems.at[place], device_id=(g + dx, s + dy), device_id_type=MESH,
        )

    halo = []
    for place, (dx, dy) in enumerate(directions):
        from_x, to_x = span(dx, nx, 2)
        from_y, to_y = span(dy, ny, pad_y)
        halo.append((
            dx, dy,
            remote(vel.at[:, from_x, from_y, :], u.at[:, to_x, to_y, :], place, dx, dy),
        ))
    memory = []
    place = len(directions)
    for dy in (1, -1):
        side = 0 if dy > 0 else 1
        columns = pl.ds(ny - reach, reach) if dy > 0 else pl.ds(0, reach)
        for number, field in enumerate((lm_in, mm_in)):
            memory.append((0, dy, remote(
                field.at[:, columns, :], raw.at[number, :, pl.ds(side * reach, reach), :], place, 0, dy
            )))
            place += 1
        memory.append((0, dy, remote(ids.at[0, 0], lists.at[side], place, 0, dy)))
        place += 1

    incoming = (
        ((g > 0).astype(jnp.int32) + (g < groups - 1).astype(jnp.int32) + 1)
        * ((s > 0).astype(jnp.int32) + (s < peers - 1).astype(jnp.int32) + 1)
        - 1
    )
    pl.semaphore_wait(barrier, incoming)
    for dx, dy, copy in halo + memory:
        @pl.when(has(dx, dy))
        def _(copy=copy):
            copy.start()

    for copy in own_copies:
        copy.wait()
    lines = 4 * nx
    blocks = nx * ny
    slot_rows = slots[...].astype(jnp.float32).reshape(lines, 1, ny)
    lane = lax.broadcasted_iota(jnp.int32, (1, ny, ny), 2)
    edge_row = lax.broadcasted_iota(jnp.int32, (1, 2 * reach, ny), 1)
    edge_row = jnp.where(edge_row < reach, edge_row, edge_row + ny - 2 * reach)

    def slot_column(wanted):
        picks = jnp.where(lane[:, : wanted.shape[1]] == wanted, slot_rows, 0.0)
        return jnp.sum(picks, axis=2, keepdims=True)

    def one_hot(column, begin, count):
        ids_of = (lax.broadcasted_iota(jnp.int32, (1, 1, count), 2) + begin).astype(jnp.float32)
        hot = jnp.where(column == ids_of, 1.0, 0.0)
        hot = hot.reshape(lines * column.shape[1], count).astype(jnp.bfloat16)
        return jnp.concatenate([hot, hot], axis=1)

    own_table = jnp.concatenate([lm[...].reshape(blocks, nz), mm[...].reshape(blocks, nz)], axis=1)
    own_hot = one_hot(slot_column(lax.broadcasted_iota(jnp.int32, (1, ny, ny), 1)), 0, blocks)
    picked[...] = jnp.dot(own_hot, halves(own_table), preferred_element_type=jnp.float32)
    capacity = lists.shape[2]
    far_hot = one_hot(slot_column(edge_row), blocks, 2 * capacity)
    weight_copy.wait()

    def own_step(x, carry):
        for half in range(ny // 8):
            moved = [None, None]
            for corner in range(4):
                low = w[2 * corner, x, half * 8 : half * 8 + 8, :]
                high = w[2 * corner + 1, x, half * 8 : half * 8 + 8, :]
                start = pl.multiple_of((corner * nx + x) * ny, ny) + half * 8
                for field in range(2):
                    base = picked[pl.ds(pl.multiple_of(start, 8), 8), field * nz : (field + 1) * nz]
                    term = low * base + high * pltpu.roll(base, nz - 1, 1)
                    moved[field] = term if moved[field] is None else moved[field] + term
            for field in range(2):
                own_moved[field, x, half * 8 : half * 8 + 8, :] = moved[field]
        return carry

    lax.fori_loop(0, nx, own_step, 0)

    own_vel.wait()
    for dx, dy, copy in halo:
        @pl.when(has(-dx, -dy))
        def _(copy=copy):
            copy.wait_recv()

    row = lax.broadcasted_iota(jnp.int32, (8, nz), 0)
    chunks = raws.shape[2] // 8
    insides = []
    for chunk in range(chunks):
        low = jnp.where((row + 8 * chunk > 0) | (s > 0), 1.0, 0.0)
        insides.append(jnp.where((row + 8 * chunk < ny + 1) | (s < peers - 1), low, 0.0))

    def strain_at(e, slot):
        shift = e // 1024
        within = jnp.where(((e > 0) | (g > 0)) & ((e < nx + 1) | (g < groups - 1)), 1.0, 0.0)
        def get(comp, along_x, along_y, count):
            return u[comp, e + 1 + along_x, pl.ds(pad_y - 1 + along_y + shift, count), :]
        for chunk in range(chunks):
            k = 8 * chunk
            center = [get(comp, 0, k, 8) for comp in range(3)]
            slopes = [
                [get(comp, 1, k, 8) - get(comp, -1, k, 8) for comp in range(3)],
                [get(comp, 0, k + 1, 8) - get(comp, 0, k - 1, 8) for comp in range(3)],
                [pltpu.roll(center[comp], nz - 1, 1) - pltpu.roll(center[comp], 1, 1) for comp in range(3)],
            ]
            mask = insides[chunk] * within
            parts = [(slopes[b][a] + slopes[a][b]) * mask for a, b in pair_list]
            total = parts[0] * parts[0] + parts[1] * parts[1] + parts[2] * parts[2]
            total = total + 2.0 * (parts[3] * parts[3] + parts[4] * parts[4] + parts[5] * parts[5])
            mag = root(total * 0.125 + 1e-06)
            mags[e, k : k + 8, :] = mag
            for place in range(6):
                a, b = pair_list[place]
                raws[slot, place, k : k + 8, :] = parts[place]
                raws[slot, 6 + place, k : k + 8, :] = mag * parts[place]
                raws[slot, 12 + place, k : k + 8, :] = center[a] * center[b]
        for place in range(18):
            below = raws[slot, place, pl.ds(shift, ny), :]
            middle = raws[slot, place, pl.ds(shift + 1, ny), :]
            above = raws[slot, place, pl.ds(shift + 2, ny), :]
            smooth[place, e] = (below + above) + (middle + middle)
        for comp in range(3):
            middle = get(comp, 0, 1, ny)
            smooth[18 + comp, e] = (get(comp, 0, 0, ny) + get(comp, 0, 2, ny)) + (middle + middle)

    def strain_step(i, carry):
        for slot in range(raws.shape[0]):
            strain_at(i * raws.shape[0] + slot, slot)
        return carry

    lax.fori_loop(0, (nx + 2) // raws.shape[0], strain_step, 0)

    for dx, dy, copy in memory:
        @pl.when(has(-dx, -dy))
        def _(copy=copy):
            copy.wait_recv()
    strip = nx * 2 * reach
    near = jnp.concatenate([raw[0].reshape(strip, nz), raw[1].reshape(strip, nz)], axis=1)
    near = halves(near)
    line = lax.broadcasted_iota(jnp.int32, (strip, capacity), 0)
    column = line % (2 * reach)
    line_row = line // (2 * reach)
    below_id = jnp.where(column < reach, line_row * ny + (ny - reach) + column, -5)
    above_id = jnp.where(column >= reach, line_row * ny + column - reach, -5)
    listed = []
    for side, block_id in ((0, below_id), (1, above_id)):
        hot = jnp.where(block_id == lists[side, side : side + 1, :], 1.0, 0.0).astype(jnp.bfloat16)
        hot = jnp.concatenate([hot, hot], axis=0)
        listed.append(lax.dot_general(hot, near, (((0,), (0,)), ((), ())), preferred_element_type=jnp.float32))
    far_table = halves(jnp.concatenate(listed, axis=0))
    far_picked[...] = jnp.dot(far_hot, far_table, preferred_element_type=jnp.float32)
    edge_low = lax.broadcasted_iota(jnp.int32, (8, nz), 0) < reach

    def final_step(x, carry):
        shift = x // 1024
        def filtered(half, place):
            ys = slice(half * 8, half * 8 + 8)
            f = (smooth[place, x, ys] + smooth[place, x + 2, ys]) + 2.0 * smooth[place, x + 1, ys]
            return (pltpu.roll(f, 1, 1) + pltpu.roll(f, nz - 1, 1)) + (f + f)
        far = [None, None]
        for corner in range(4):
            low = jnp.where(edge_low, w[2 * corner, x, 0:8, :], w[2 * corner, x, ny - 8 : ny, :])
            high = jnp.where(edge_low, w[2 * corner + 1, x, 0:8, :], w[2 * corner + 1, x, ny - 8 : ny, :])
            start = pl.multiple_of((corner * nx + x) * 8, 8)
            for field in range(2):
                base = far_picked[pl.ds(start, 8), field * nz : (field + 1) * nz]
                term = low * base + high * pltpu.roll(base, nz - 1, 1)
                far[field] = term if far[field] is None else far[field] + term
        for half in range(ny // 8):
            ys = slice(half * 8, half * 8 + 8)
            def keep(value):
                return jnp.where(edge_low, value, 0.0) if half == 0 else jnp.where(edge_low, 0.0, value)
            flow = [0.125 * filtered(half, 18 + comp) for comp in range(3)]
            parts = [filtered(half, place) for place in range(6)]
            total = parts[0] * parts[0] + parts[1] * parts[1] + parts[2] * parts[2]
            total = total + 2.0 * (parts[3] * parts[3] + parts[4] * parts[4] + parts[5] * parts[5])
            mag4 = 4.0 * root(total * (2.0 / 65536.0) + 1e-06)
            lm_sum, mm_sum = [], []
            for group in (range(3), range(3, 6)):
                lm_part = mm_part = None
                for place in group:
                    a, b = pair_list[place]
                    leonard = filtered(half, 12 + place) - flow[a] * flow[b]
                    model = filtered(half, 6 + place) - mag4 * parts[place]
                    lm_part = leonard * model if lm_part is None else lm_part + leonard * model
                    mm_part = model * model if mm_part is None else mm_part + model * model
                lm_sum.append(lm_part)
                mm_sum.append(mm_part)
            lm_local = (lm_sum[0] + 2.0 * lm_sum[1]) * (1.0 / 8192.0)
            mm_local = (mm_sum[0] + 2.0 * mm_sum[1]) * (1.0 / 16384.0)
            moved_lm = own_moved[0, x, ys, :] + keep(far[0])
            moved_mm = own_moved[1, x, ys, :] + keep(far[1])
            power = root(root(root(jnp.maximum(jnp.maximum(moved_lm, 0.0) * moved_mm, floor_value))))
            rate = (time_step / 1.5) * power
            blend = rate / (1.0 + rate)
            new_lm = jnp.maximum(moved_lm + blend * (lm_local - moved_lm), 0.0)
            new_mm = moved_mm + blend * (mm_local - moved_mm)
            outs[0, x, ys, :] = new_lm
            outs[1, x, ys, :] = new_mm
            outs[2, x, ys, :] = new_lm / new_mm * mags[x + 1, pl.ds(half * 8 + 1 + shift, 8), :]
        return carry

    sent = []
    unroll = nx // 2
    for part in range(2):
        strip_x = pl.ds(part * (nx // 2), nx // 2)
        lax.fori_loop(part * (nx // 2), (part + 1) * (nx // 2), final_step, 0, unroll=unroll)
        for place, target in enumerate((new_lm_out, new_mm_out, visc_out)):
            copy = pltpu.make_async_copy(outs.at[place, strip_x], target.at[strip_x], out_sems.at[part, place])
            copy.start()
            sent.append(copy)

    for dx, dy, copy in halo + memory:
        @pl.when(has(dx, dy))
        def _(copy=copy):
            copy.wait_send()
    for copy in sent:
        copy.wait()


def hand_over(a_in, b_in, c_in, a_out, b_out, c_out, held, in_sems, out_sems):
    arrivals, departures = [], []
    for place, (source, target) in enumerate(((a_in, a_out), (b_in, b_out), (c_in, c_out))):
        arrivals.append(pltpu.make_async_copy(source, held.at[place], in_sems.at[place]))
        departures.append(pltpu.make_async_copy(held.at[place], target, out_sems.at[place]))
    for copy in arrivals:
        copy.start()
    for arrival, departure in zip(arrivals, departures):
        arrival.wait()
        departure.start()
    for copy in departures:
        copy.wait()


def on_device(velocity, mem_lm, mem_mm, send_ids, read_slot, weights):
    nx, ny, nz = mem_lm.shape
    capacity = send_ids.shape[3]
    f32 = jnp.float32
    rows = ny + 8
    out = jax.ShapeDtypeStruct(mem_lm.shape, f32)
    copies = len(directions) + 6
    fields = pl.pallas_call(
        kernel,
        out_shape=(out, out, out),
        in_specs=[pl.BlockSpec(memory_space=pltpu.HBM)] * 6,
        out_specs=[pl.BlockSpec(memory_space=pltpu.HBM)] * 3,
        scratch_shapes=[
            pltpu.VMEM((3, nx + 4, ny + 2 * pad_y, nz), f32),
            pltpu.VMEM(mem_lm.shape, f32),
            pltpu.VMEM(mem_lm.shape, f32),
            pltpu.VMEM(read_slot.shape, jnp.int32),
            pltpu.VMEM(weights.shape, f32),
            pltpu.VMEM((2, nx, 2 * reach, nz), f32),
            pltpu.VMEM((2, 2, capacity), jnp.int32),
            pltpu.VMEM((4 * nx * ny, 2 * nz), f32),
            pltpu.VMEM((4 * nx * 2 * reach, 2 * nz), f32),
            pltpu.VMEM((2,) + mem_lm.shape, f32),
            pltpu.VMEM((6, 18, rows, nz), f32),
            pltpu.VMEM((nx + 2, rows, nz), f32),
            pltpu.VMEM((21, nx + 2, ny, nz), f32),
            pltpu.VMEM((3,) + mem_lm.shape, f32),
            pltpu.SemaphoreType.DMA((copies,)),
            pltpu.SemaphoreType.DMA((copies,)),
            pltpu.SemaphoreType.DMA((5,)),
            pltpu.SemaphoreType.DMA((2, 3)),
        ],
        compiler_params=pltpu.CompilerParams(
            collective_id=0, has_side_effects=True, vmem_limit_bytes=60 << 20
        ),
    )(velocity, mem_lm, mem_mm, send_ids, read_slot, weights)
    return pl.pallas_call(
        hand_over,
        out_shape=(out, out, out),
        in_specs=[pl.BlockSpec(memory_space=pltpu.HBM)] * 3,
        out_specs=[pl.BlockSpec(memory_space=pltpu.HBM)] * 3,
        scratch_shapes=[
            pltpu.VMEM((3,) + mem_lm.shape, f32),
            pltpu.SemaphoreType.DMA((3,)),
            pltpu.SemaphoreType.DMA((3,)),
        ],
        compiler_params=pltpu.CompilerParams(vmem_limit_bytes=60 << 20),
    )(*fields)


def solution(mesh):
    return jax.shard_map(
        on_device,
        mesh=mesh,
        in_specs=(
            P(None, "age", "slab", None),
            P("age", "slab", None),
            P("age", "slab", None),
            P("age", "slab", None, None),
            P(None, "age", "slab"),
            P(None, "age", "slab", None),
        ),
        out_specs=(P("age", "slab", None), P("age", "slab", None), P("age", "slab", None)),
        check_vma=False,
    )
```
